32 devices in a mesh: lat: 4 (over x, core), lon: 8 (over z, y).
Axes of the slice: x: 2, y: 2, z: 4, core: 2. Of those that a mesh axis runs over, the one named last changes fastest.
Arguments:
- features: bfloat16 [8, 128, 256, 256], P(None, 'lat', 'lon'), may hold values from -16 to 16
- band_points: int32 [128], replicated, may hold values from 64 to 256, as said below
- survival_flags: int32 [8, 2], replicated, may hold values 0 or 1
- first_kernel_weight: bfloat16 [3, 3, 256, 256], replicated, may hold values from -0.125 to 0.125
- second_kernel_weight: bfloat16 [3, 3, 256, 256], replicated, may hold values from -0.125 to 0.125
Outputs:
- section_result: bfloat16 [8, 128, 256, 256], P(None, 'lat', 'lon')
The draws below stay inside these ranges and needn't reach their ends.
Inputs may be any that keep to these rules, and one draw needn't show every extreme that they name: `band_points`: the live points of a row are its first ones.
All inputs are finite; a program needn't handle non-finite values.
Results may differ from the reference program's by a relative error of at most 0.0006.
The reference program's roundings to bfloat16 on the way count: a program that leaves them out, or rounds other values in their place, can miss the bound.
Values may be sent and summed in bfloat16 or wider, within the bound.
A program may use at most 320 MiB of HBM per device.

```python
import math
import jax
import jax.numpy as jnp
from jax import lax

C = 256
GROUPS = 32
FIRST_DILATION = 2
SECOND_DILATION = 4
B = 8
NLAT = 128
NLON = 256


def draw_band_points(key, part):
    counts = jax.random.randint(key, (NLAT,), NLON // 4, NLON + 1)
    counts = counts.at[NLAT // 2].set(NLON)
    return counts.at[0].set(NLON // 4).astype(jnp.int32)


def draw_features(key, part):
    keys = jax.random.split(key, 4)
    col_ramp = 0.6 + 1.2 * jnp.arange(NLON, dtype=jnp.float32) / (NLON - 1)
    chan_scale = jnp.exp(jax.random.uniform(keys[1], (C,), minval=math.log(0.3), maxval=math.log(3.0)))
    cell_scale = jnp.exp(jax.random.uniform(keys[2], (B, NLAT, NLON, 1), minval=-0.4, maxval=0.4))
    offset = jax.random.normal(keys[3], (C,)) * 0.5
    noise = jax.random.normal(keys[0], (B, NLAT, NLON, C))
    values = (noise * cell_scale * chan_scale + offset) * col_ramp[:, None]
    return jnp.clip(values, -16.0, 16.0).astype(jnp.bfloat16)


def touch_ends(array, key, low, top_value):
    dims = array.shape
    index_at = [jax.random.randint(jax.random.fold_in(key, axis), (), 0, dims[axis]) for axis in range(len(dims))]
    array = array.at[tuple(index_at)].set(low)
    longest = dims.index(max(dims))
    index_at[longest] = (index_at[longest] + 1) % dims[longest]
    return array.at[tuple(index_at)].set(top_value)


def centred(own_key, extent, scale, bound, kind=jnp.bfloat16):
    array = scale * jax.random.normal(own_key, extent, jnp.float32)
    return jnp.clip(array, min=-bound, max=bound).astype(kind)


def setup_inputs(seed: int = 0) -> dict:
    arg_keys = jax.random.split(jax.random.key(seed), 6)
    return {
        "features": draw_features(jax.random.fold_in(arg_keys[5], 71), 0),
        "band_points": draw_band_points(jax.random.fold_in(arg_keys[5], 71), 0),
        "survival_flags": touch_ends((jax.random.randint(arg_keys[2], (B, 2), 0, 5) < 4).astype(jnp.int32), jax.random.fold_in(arg_keys[2], 1), 0, 1),
        "first_kernel_weight": centred(arg_keys[3], (3, 3, C, C), (9 * C) ** -0.5, 0.125),
        "second_kernel_weight": centred(arg_keys[4], (3, 3, C, C), (9 * C) ** -0.5, 0.125),
    }


EPS = 1e-05
KEEP_RATE = 0.8

def activate(field_in, live_mask, live_count, group_size):
    samples = field_in.shape[0]
    masked = field_in * live_mask[None, :, :, None]
    group_means = lax.optimization_barrier(jnp.sum(masked, axis=(1, 2))).reshape(samples, GROUPS, group_size).sum(axis=2) / live_count
    shifted = field_in - jnp.repeat(group_means, group_size, axis=1)[:, None, None, :]
    squares = shifted * shifted * live_mask[None, :, :, None]
    group_vars = lax.optimization_barrier(jnp.sum(squares, axis=(1, 2))).reshape(samples, GROUPS, group_size).sum(axis=2) / live_count
    inv_std = jnp.repeat(lax.rsqrt(group_vars + EPS), group_size, axis=1)[:, None, None, :]
    return (jax.nn.silu(shifted * inv_std) * live_mask[None, :, :, None]).astype(jnp.bfloat16)

def apply_kernel(acts, weight, dilation):
    lat_total = acts.shape[1]
    lon_total = acts.shape[2]

    def one_sample(plane):
        wrapped = jnp.concatenate([plane[:, lon_total - dilation:], plane, plane[:, :dilation]], axis=1)
        padded = jnp.pad(wrapped, ((dilation, dilation), (0, 0), (0, 0)))
        summed = jnp.zeros((lat_total, lon_total, weight.shape[3]), jnp.float32)
        for row_tap in range(3):
            for col_tap in range(3):
                shifted = padded[row_tap * dilation:row_tap * dilation + lat_total, col_tap * dilation:col_tap * dilation + lon_total]
                summed = summed + jnp.einsum('ijc,cd->ijd', shifted.astype(jnp.float32), weight[row_tap, col_tap].astype(jnp.float32))
        return summed
    return lax.map(one_sample, acts)

def reference(features, band_points, survival_flags, first_kernel_weight, second_kernel_weight):
    lon_total = features.shape[2]
    channels = features.shape[3]
    group_size = channels // GROUPS
    live_mask = (jnp.arange(lon_total, dtype=jnp.int32)[None, :] < band_points[:, None]).astype(jnp.float32)
    live_count = jnp.sum(band_points).astype(jnp.float32) * group_size
    initial_feature_map = features.astype(jnp.float32)
    first_survival = survival_flags[:, 0].astype(jnp.float32) / KEEP_RATE
    second_survival = survival_flags[:, 1].astype(jnp.float32) / KEEP_RATE
    first_hidden = activate(initial_feature_map, live_mask, live_count, group_size)
    first_result = (initial_feature_map + first_survival[:, None, None, None] * apply_kernel(first_hidden, first_kernel_weight, FIRST_DILATION)).astype(jnp.bfloat16)
    first_result = lax.optimization_barrier(first_result)
    first_feature_map = first_result.astype(jnp.float32)
    second_hidden = activate(first_feature_map, live_mask, live_count, group_size)
    section_result = first_feature_map + second_survival[:, None, None, None] * apply_kernel(second_hidden, second_kernel_weight, SECOND_DILATION)
    return section_result.astype(jnp.bfloat16)
```

```python
import functools

import jax
import jax.numpy as jnp
from jax import lax
from jax.experimental import pallas as pl
from jax.experimental.pallas import tpu as pltpu
from jax.sharding import PartitionSpec as P

GROUPS = 32
DILATIONS = (2, 4)
EPS = 1e-05
KEEP_RATE = 0.8
LANES = 128
ROWS_PER_STEP = 2
MESH = pl.DeviceIdType.MESH
HIGHEST = lax.Precision.HIGHEST


def kernel(
    n_lat, n_lon, tile_rows, tile_cols, samples, channels,
    feat_ref, points_ref, flags_ref, w1_ref, w2_ref, out_ref,
    x_ref, pad1, pad2, mine, lat_slots, lon_slots,
    stat_send, stat_recv, halo_send, halo_recv,
):
    cells = tile_cols * samples
    group_size = channels // GROUPS
    lat = lax.axis_index("lat")
    lon = lax.axis_index("lon")
    row0 = lat * tile_rows
    col0 = lon * tile_cols

    barrier = pltpu.get_barrier_semaphore()
    for k in range(1, n_lat):
        pl.semaphore_signal(
            barrier, inc=1, device_id={"lat": lax.rem(lat + k, n_lat)}, device_id_type=MESH
        )
    for k in range(1, n_lon):
        pl.semaphore_signal(
            barrier, inc=1, device_id={"lon": lax.rem(lon + k, n_lon)}, device_id_type=MESH
        )

    def live(row, first, width):
        column = lax.broadcasted_iota(jnp.int32, (width, channels), 0) // samples
        return column + (first // samples + col0) < points_ref[row0 + row]

    def per_sample(values):
        return values.reshape(-1, samples, channels).sum(axis=0)

    member = (
        lax.broadcasted_iota(jnp.int32, (channels, LANES), 0) // group_size
        == lax.broadcasted_iota(jnp.int32, (channels, LANES), 1)
    ).astype(jnp.float32)
    spread_map = (
        lax.broadcasted_iota(jnp.int32, (LANES, channels), 1) // group_size
        == lax.broadcasted_iota(jnp.int32, (LANES, channels), 0)
    ).astype(jnp.float32)

    def group_total(values):
        return jnp.dot(values, member, precision=HIGHEST, preferred_element_type=jnp.float32)

    def spread(values):
        return jnp.dot(values, spread_map, precision=HIGHEST, preferred_element_type=jnp.float32)

    def count_row(i, total):
        return total + jnp.clip(points_ref[row0 + i] - col0, 0, tile_cols)

    local_cells = lax.fori_loop(0, tile_rows, count_row, jnp.int32(0))
    local_count = jnp.full((samples, LANES), local_cells * group_size, jnp.int32).astype(
        jnp.float32
    )

    def combine(parts):
        total = sum(p[0] for p in parts)
        count = sum(p[2] for p in parts)
        mean = total / jnp.maximum(count, 1.0)
        spreads = None
        for p in parts:
            gap = p[0] / jnp.maximum(p[2], 1.0) - mean
            term = p[1] + p[2] * gap * gap
            spreads = term if spreads is None else spreads + term
        return total, spreads, count, mean

    def exchange(round_index, stage, axis, index, peers, slots):
        copies = []
        base = (round_index * 2 + stage) * max(n_lat, n_lon)
        for k in range(1, peers):
            copy = pltpu.make_async_remote_copy(
                src_ref=mine.at[round_index, stage],
                dst_ref=slots.at[round_index, k],
                send_sem=stat_send.at[base + k],
                recv_sem=stat_recv.at[base + k],
                device_id={axis: lax.rem(index + k, peers)},
                device_id_type=MESH,
            )
            copy.start()
            copies.append(copy)
        for copy in copies:
            copy.wait()
        parts = [tuple(mine[round_index, stage, j] for j in range(3))]
        for k in range(1, peers):
            parts.append(tuple(slots[round_index, k, j] for j in range(3)))
        return combine(parts)

    def sum_row(i, total):
        values = x_ref[i].astype(jnp.float32)
        return total + per_sample(jnp.where(live(i, 0, cells), values, 0.0))

    def load_row(i, total):
        values = jnp.swapaxes(feat_ref[:, i].astype(jnp.float32), 0, 1)
        values = values.reshape(cells, channels)
        x_ref[i] = values.astype(jnp.bfloat16)
        return total + per_sample(jnp.where(live(i, 0, cells), values, 0.0))

    def local_statistics(round_index, row_body):
        zero = jnp.zeros((samples, channels), jnp.float32)
        total = group_total(lax.fori_loop(0, tile_rows, row_body, zero))
        mean = spread(total / jnp.maximum(local_count, 1.0))

        def square_row(i, acc):
            values = x_ref[i].astype(jnp.float32).reshape(tile_cols, samples, channels)
            gap = (values - mean[None]).reshape(cells, channels)
            return acc + per_sample(jnp.where(live(i, 0, cells), gap * gap, 0.0))

        squares = group_total(lax.fori_loop(0, tile_rows, square_row, zero))
        mine[round_index, 0, 0] = total
        mine[round_index, 0, 1] = squares
        mine[round_index, 0, 2] = local_count

    def global_statistics(round_index):
        total, squares, count, _ = exchange(round_index, 0, "lat", lat, n_lat, lat_slots)
        mine[round_index, 1, 0] = total
        mine[round_index, 1, 1] = squares
        mine[round_index, 1, 2] = count
        total, squares, count, mean = exchange(round_index, 1, "lon", lon, n_lon, lon_slots)
        inv_std = lax.rsqrt(squares / jnp.maximum(count, 1.0) + EPS)
        return spread(mean), spread(inv_std) * 0.5

    def block(round_index, pad, w_ref, mean, half_scale):
        d = DILATIONS[round_index]
        side = d * samples
        rows = tile_rows

        def act(i, first, width):
            values = x_ref[i, pl.ds(first, width), :].astype(jnp.float32)
            values = values.reshape(width // samples, samples, channels)
            half = ((values - mean[None]) * half_scale[None]).reshape(width, channels)
            hidden = half * jnp.tanh(half) + half
            hidden = jnp.where(live(i, first, width), hidden, 0.0)
            pad[d + i, pl.ds(side + first, width), :] = hidden.astype(jnp.bfloat16)

        def remote(number, src, dst, target):
            return pltpu.make_async_remote_copy(
                src_ref=src,
                dst_ref=dst,
                send_sem=halo_send.at[round_index * 8 + number],
                recv_sem=halo_recv.at[round_index * 8 + number],
                device_id=target,
                device_id_type=MESH,
            )

        middle = pl.ds(side, cells)
        up = {"lat": lax.rem(lat + n_lat - 1, n_lat)}
        down = {"lat": lax.rem(lat + 1, n_lat)}
        right = {"lon": lax.rem(lon + 1, n_lon)}
        left = {"lon": lax.rem(lon + n_lon - 1, n_lon)}
        to_up = remote(0, pad.at[pl.ds(d, d), middle], pad.at[pl.ds(d + rows, d), middle], up)
        to_down = remote(1, pad.at[pl.ds(rows, d), middle], pad.at[pl.ds(0, d), middle], down)

        def sideways(number, first, height):
            span = pl.ds(first, height)
            return [
                remote(
                    number, pad.at[span, pl.ds(cells, side)], pad.at[span, pl.ds(0, side)], right
                ),
                remote(
                    number + 1,
                    pad.at[span, pl.ds(side, side)],
                    pad.at[span, pl.ds(side + cells, side)],
                    left,
                ),
            ]

        flanks = sideways(2, d, rows)
        corners = sideways(4, 0, d) + sideways(6, d + rows, d)

        @pl.loop(0, d)
        def _(i):
            act(i, 0, cells)
            act(rows - d + i, 0, cells)

        @pl.when(lat > 0)
        def _():
            to_up.start()

        @pl.when(lat < n_lat - 1)
        def _():
            to_down.start()

        @pl.loop(d, rows - d)
        def _(i):
            act(i, 0, side)
            act(i, cells - side, side)

        for copy in flanks:
            copy.start()

        @pl.loop(d, rows - d)
        def _(i):
            act(i, side, cells - 2 * side)

        @pl.when(lat == 0)
        def _():
            pad[pl.ds(0, d), middle, :] = jnp.zeros((d, cells, channels), jnp.bfloat16)

        @pl.when(lat == n_lat - 1)
        def _():
            pad[pl.ds(d + rows, d), middle, :] = jnp.zeros((d, cells, channels), jnp.bfloat16)

        @pl.when(lat > 0)
        def _():
            to_down.wait_recv()
            to_up.wait_send()

        @pl.when(lat < n_lat - 1)
        def _():
            to_up.wait_recv()
            to_down.wait_send()

        for copy in corners:
            copy.start()

        sample_index = lax.broadcasted_iota(jnp.int32, (samples, channels), 0)
        flag = jnp.zeros((samples, channels), jnp.int32)
        for s in range(samples):
            flag = jnp.where(sample_index == s, flags_ref[s, round_index], flag)
        kept = flag.astype(jnp.float32) / KEEP_RATE

        def conv(first_row, height, first, width):
            taps = [
                pad[
                    pl.ds(first_row + r * d, height), pl.ds(first + c * side, width), :
                ].reshape(height * width, channels)
                for r in range(3)
                for c in range(3)
            ]
            summed = jnp.dot(
                jnp.concatenate(taps, axis=1), w_ref[...], preferred_element_type=jnp.float32
            )
            summed = summed.reshape(height * width // samples, samples, channels) * kept[None]
            where = (pl.ds(first_row, height), pl.ds(first, width), slice(None))
            old = x_ref[where].astype(jnp.float32)
            x_ref[where] = (old + summed.reshape(height, width, channels)).astype(jnp.bfloat16)

        @pl.loop(0, tile_rows // ROWS_PER_STEP)
        def _(step):
            conv(step * ROWS_PER_STEP, ROWS_PER_STEP, side, cells - 2 * side)

        for copy in flanks + corners:
            copy.wait()

        strip_rows = 512 // side

        @pl.loop(0, tile_rows // strip_rows)
        def _(step):
            conv(step * strip_rows, strip_rows, 0, side)
            conv(step * strip_rows, strip_rows, cells - side, side)

    local_statistics(0, load_row)
    pl.semaphore_wait(barrier, n_lat - 1 + n_lon - 1)
    block(0, pad1, w1_ref, *global_statistics(0))
    local_statistics(1, sum_row)
    block(1, pad2, w2_ref, *global_statistics(1))

    @pl.loop(0, tile_rows)
    def _(i):
        values = x_ref[i].astype(jnp.float32).reshape(tile_cols, samples, channels)
        out_ref[:, i] = jnp.swapaxes(values, 0, 1).astype(jnp.bfloat16)


def per_device(n_lat, n_lon, features, band_points, survival_flags, first_weight, second_weight):
    samples, rows, cols, channels = features.shape
    d1, d2 = DILATIONS
    vmem = pl.BlockSpec(memory_space=pltpu.VMEM)
    smem = pl.BlockSpec(memory_space=pltpu.SMEM)
    message = (3, samples, LANES)
    slots = 4 * max(n_lat, n_lon)
    taps = (9 * channels, channels)

    def padded(d):
        shape = (rows + 2 * d, (cols + 2 * d) * samples, channels)
        return pltpu.VMEM(shape, jnp.bfloat16)

    return pl.pallas_call(
        functools.partial(kernel, n_lat, n_lon, rows, cols, samples, channels),
        out_shape=jax.ShapeDtypeStruct(features.shape, jnp.bfloat16),
        in_specs=[vmem, smem, smem, vmem, vmem],
        out_specs=vmem,
        scratch_shapes=[
            pltpu.VMEM((rows, cols * samples, channels), jnp.bfloat16),
            padded(d1),
            padded(d2),
            pltpu.VMEM((2, 2) + message, jnp.float32),
            pltpu.VMEM((2, n_lat) + message, jnp.float32),
            pltpu.VMEM((2, n_lon) + message, jnp.float32),
            pltpu.SemaphoreType.DMA((slots,)),
            pltpu.SemaphoreType.DMA((slots,)),
            pltpu.SemaphoreType.DMA((16,)),
            pltpu.SemaphoreType.DMA((16,)),
        ],
        compiler_params=pltpu.CompilerParams(
            collective_id=0, has_side_effects=True, vmem_limit_bytes=56 * 2**20
        ),
    )(
        features,
        band_points,
        survival_flags,
        first_weight.reshape(taps),
        second_weight.reshape(taps),
    )


def solution(mesh):
    in_specs = (P(None, "lat", "lon", None), P(), P(), P(), P())
    out_specs = P(None, "lat", "lon", None)
    return jax.shard_map(
        functools.partial(per_device, mesh.shape["lat"], mesh.shape["lon"]),
        mesh=mesh,
        in_specs=in_specs,
        out_specs=out_specs,
        check_vma=False,
    )
```

```python
import functools

import jax
import jax.numpy as jnp
from jax import lax
from jax.experimental import pallas as pl
from jax.experimental.pallas import tpu as pltpu
from jax.sharding import PartitionSpec as P

GROUPS = 32
DILATIONS = (2, 4)
EPS = 1e-05
KEEP_RATE = 0.8
LANES = 128
ROWS_PER_STEP = 4
LOAD_CHUNKS = 4
MESH = pl.DeviceIdType.MESH


def kernel(
    n_lat, n_lon, tile_rows, tile_cols, samples, channels,
    feat_hbm, points_ref, flags_ref, w1_hbm, w2_hbm, x_ref,
    feat_ref, w1_ref, w2_ref, pad1, pad2, total_ref, mine, lat_slots, lon_slots,
    local_sem, stat_send, stat_recv, halo_send, halo_recv,
):
    cells = tile_cols * samples
    group_size = channels // GROUPS
    lat = lax.axis_index("lat")
    lon = lax.axis_index("lon")
    row0 = lat * tile_rows
    col0 = lon * tile_cols

    chunk = tile_rows // LOAD_CHUNKS
    loads = []
    for c in range(LOAD_CHUNKS):
        part = (slice(None), pl.ds(c * chunk, chunk))
        loads.append((feat_hbm.at[part], feat_ref.at[part]))
    loads += [(w1_hbm, w1_ref), (w2_hbm, w2_ref)]
    loads = [pltpu.make_async_copy(*ends, local_sem.at[k]) for k, ends in enumerate(loads)]
    for copy in loads:
        copy.start()

    barrier = pltpu.get_barrier_semaphore()
    for k in range(1, n_lat):
        pl.semaphore_signal(
            barrier, inc=1, device_id={"lat": lax.rem(lat + k, n_lat)}, device_id_type=MESH
        )
    for k in range(1, n_lon):
        pl.semaphore_signal(
            barrier, inc=1, device_id={"lon": lax.rem(lon + k, n_lon)}, device_id_type=MESH
        )

    def live(row, first, width):
        shape = (width // samples, samples, channels)
        column = lax.broadcasted_iota(jnp.int32, shape, 0)
        return column + (first // samples + col0) < points_ref[row0 + row]

    def cubed(values):
        return values.reshape(-1, samples, channels)

    halves = channels // LANES

    def pack(values):
        return jnp.concatenate(jnp.split(values, halves, axis=1), axis=0)

    def unpack(values):
        return jnp.concatenate(jnp.split(values, halves, axis=0), axis=1)

    lane = lax.broadcasted_iota(jnp.int32, (halves * samples, LANES), 1)
    place = lane % group_size

    def group_total(values):
        step = 1
        while step < group_size:
            above = pltpu.roll(values, LANES - step, 1)
            below = pltpu.roll(values, step, 1)
            values = values + jnp.where((lane & step) == 0, above, below)
            step *= 2
        return values

    def spread(values):
        return unpack(group_total(jnp.where(place == 0, values, 0.0)))

    def message(total, squares, count):
        return jnp.where(place == 0, total, jnp.where(place == 1, squares, count))

    def count_row(i, total):
        return total + jnp.clip(points_ref[row0 + i] - col0, 0, tile_cols)

    local_cells = lax.fori_loop(0, tile_rows, count_row, jnp.int32(0))
    local_count = jnp.full((halves * samples, LANES), local_cells * group_size, jnp.int32).astype(
        jnp.float32
    )

    def combine(parts):
        total = sum(p[0] for p in parts)
        count = sum(p[2] for p in parts)
        mean = total / jnp.maximum(count, 1.0)
        spreads = None
        for p in parts:
            gap = p[0] / jnp.maximum(p[2], 1.0) - mean
            term = p[1] + p[2] * gap * gap
            spreads = term if spreads is None else spreads + term
        return total, spreads, count, mean

    def exchange(round_index, stage, axis, index, peers, slots):
        copies = []
        base = (round_index * 2 + stage) * max(n_lat, n_lon)
        for k in range(1, peers):
            copy = pltpu.make_async_remote_copy(
                src_ref=mine.at[round_index, stage],
                dst_ref=slots.at[round_index, k],
                send_sem=stat_send.at[base + k],
                recv_sem=stat_recv.at[base + k],
                device_id={axis: lax.rem(index + k, peers)},
                device_id_type=MESH,
            )
            copy.start()
            copies.append(copy)
        for copy in copies:
            copy.wait()
        packed = [mine[round_index, stage]] + [slots[round_index, k] for k in range(1, peers)]
        return combine(
            [(p, pltpu.roll(p, LANES - 1, 1), pltpu.roll(p, LANES - 2, 1)) for p in packed]
        )

    def load_row(i, total):
        values = jnp.swapaxes(feat_ref[:, i].astype(jnp.float32), 0, 1)
        x_ref[i] = values.reshape(cells, channels).astype(jnp.bfloat16)
        return total + jnp.where(live(i, 0, cells), values, 0.0).sum(axis=0)

    def local_statistics(round_index, channel_total):
        total = group_total(pack(channel_total))
        mean = unpack(total / jnp.maximum(local_count, 1.0))

        def square_row(i, acc):
            gap = cubed(x_ref[i].astype(jnp.float32)) - mean[None]
            return acc + jnp.where(live(i, 0, cells), gap * gap, 0.0).sum(axis=0)

        zero = jnp.zeros((samples, channels), jnp.float32)
        squares = group_total(pack(lax.fori_loop(0, tile_rows, square_row, zero)))
        mine[round_index, 0] = message(total, squares, local_count)

    def global_statistics(round_index):
        total, squares, count, _ = exchange(round_index, 0, "lat", lat, n_lat, lat_slots)
        mine[round_index, 1] = message(
            total, pltpu.roll(squares, 1, 1), pltpu.roll(count, 2, 1)
        )
        total, squares, count, mean = exchange(round_index, 1, "lon", lon, n_lon, lon_slots)
        inv_std = lax.rsqrt(squares / jnp.maximum(count, 1.0) + EPS)
        return spread(mean), spread(inv_std) * 0.5

    def block(round_index, pad, w_ref, weight_load, mean, half_scale):
        d = DILATIONS[round_index]
        side = d * samples
        rows = tile_rows

        def act(i, first, width):
            values = cubed(x_ref[i, pl.ds(first, width), :].astype(jnp.float32))
            half = (values - mean[None]) * half_scale[None]
            hidden = half * jnp.tanh(half) + half
            hidden = jnp.where(live(i, first, width), hidden, 0.0).reshape(width, channels)
            pad[d + i, pl.ds(side + first, width), :] = hidden.astype(jnp.bfloat16)

        def remote(number, src, dst, target):
            return pltpu.make_async_remote_copy(
                src_ref=src,
                dst_ref=dst,
                send_sem=halo_send.at[round_index * 8 + number],
                recv_sem=halo_recv.at[round_index * 8 + number],
                device_id=target,
                device_id_type=MESH,
            )

        middle = pl.ds(side, cells)
        up = {"lat": lax.rem(lat + n_lat - 1, n_lat)}
        down = {"lat": lax.rem(lat + 1, n_lat)}
        right = {"lon": lax.rem(lon + 1, n_lon)}
        left = {"lon": lax.rem(lon + n_lon - 1, n_lon)}
        to_up = remote(0, pad.at[pl.ds(d, d), middle], pad.at[pl.ds(d + rows, d), middle], up)
        to_down = remote(1, pad.at[pl.ds(rows, d), middle], pad.at[pl.ds(0, d), middle], down)

        def sideways(number, first, height):
            span = pl.ds(first, height)
            return [
                remote(
                    number, pad.at[span, pl.ds(cells, side)], pad.at[span, pl.ds(0, side)], right
                ),
                remote(
                    number + 1,
                    pad.at[span, pl.ds(side, side)],
                    pad.at[span, pl.ds(side + cells, side)],
                    left,
                ),
            ]

        flanks = sideways(2, d, rows)
        corners = sideways(4, 0, d) + sideways(6, d + rows, d)

        @pl.loop(0, d)
        def _(i):
            act(i, 0, cells)
            act(rows - d + i, 0, cells)

        @pl.when(lat > 0)
        def _():
            to_up.start()

        @pl.when(lat < n_lat - 1)
        def _():
            to_down.start()

        @pl.loop(d, rows - d)
        def _(i):
            act(i, 0, side)
            act(i, cells - side, side)

        for copy in flanks:
            copy.start()

        @pl.loop(d, rows - d)
        def _(i):
            act(i, side, cells - 2 * side)

        @pl.when(lat == 0)
        def _():
            pad[pl.ds(0, d), middle, :] = jnp.zeros((d, cells, channels), jnp.bfloat16)

        @pl.when(lat == n_lat - 1)
        def _():
            pad[pl.ds(d + rows, d), middle, :] = jnp.zeros((d, cells, channels), jnp.bfloat16)

        flag = jnp.broadcast_to(flags_ref[:, round_index : round_index + 1], (samples, channels))
        kept = flag.astype(jnp.float32) / KEEP_RATE
        weight_load.wait()

        def conv(first_row, height, first, width):
            taps = [
                pad[
                    pl.ds(first_row + r * d, height), pl.ds(first + c * side, width), :
                ].reshape(height * width, channels)
                for r in range(3)
                for c in range(3)
            ]
            summed = jnp.dot(
                jnp.concatenate(taps, axis=1), w_ref[...], preferred_element_type=jnp.float32
            )
            summed = (cubed(summed) * kept[None]).reshape(height, width, channels)
            where = (pl.ds(first_row, height), pl.ds(first, width), slice(None))
            new = (x_ref[where].astype(jnp.float32) + summed).astype(jnp.bfloat16)
            x_ref[where] = new
            if round_index == 0:
                total = total_ref[...]
                for k in range(height):
                    values = cubed(new[k].astype(jnp.float32))
                    mask = live(first_row + k, first, width)
                    total = total + jnp.where(mask, values, 0.0).sum(axis=0)
                total_ref[...] = total

        def inner(step):
            conv(step * ROWS_PER_STEP, ROWS_PER_STEP, side, cells - 2 * side)

        steps = tile_rows // ROWS_PER_STEP
        pl.loop(1, steps // 2)(inner)

        @pl.when(lat > 0)
        def _():
            to_down.wait_recv()
            to_up.wait_send()

        @pl.when(lat < n_lat - 1)
        def _():
            to_up.wait_recv()
            to_down.wait_send()

        for copy in corners:
            copy.start()

        pl.loop(steps // 2, steps - 1)(inner)
        pl.loop(0, 2)(lambda k: inner(k * (steps - 1)))

        for copy in flanks + corners:
            copy.wait()

        strip_rows = 512 // side

        @pl.loop(0, tile_rows // strip_rows)
        def _(step):
            conv(step * strip_rows, strip_rows, 0, side)
            conv(step * strip_rows, strip_rows, cells - side, side)

    total = jnp.zeros((samples, channels), jnp.float32)
    total_ref[...] = total
    for c in range(LOAD_CHUNKS):
        loads[c].wait()
        total = lax.fori_loop(c * chunk, (c + 1) * chunk, load_row, total)
    local_statistics(0, total)
    pl.semaphore_wait(barrier, n_lat - 1 + n_lon - 1)
    block(0, pad1, w1_ref, loads[LOAD_CHUNKS], *global_statistics(0))
    local_statistics(1, total_ref[...])
    block(1, pad2, w2_ref, loads[LOAD_CHUNKS + 1], *global_statistics(1))


def reorder(x_ref, out_ref):
    samples, rows, cols, channels = out_ref.shape
    for i in range(rows):
        values = x_ref[i].astype(jnp.float32).reshape(cols, samples, channels)
        out_ref[:, i] = jnp.swapaxes(values, 0, 1).astype(jnp.bfloat16)


def per_device(n_lat, n_lon, features, band_points, survival_flags, first_weight, second_weight):
    samples, rows, cols, channels = features.shape
    d1, d2 = DILATIONS
    vmem = pl.BlockSpec(memory_space=pltpu.VMEM)
    smem = pl.BlockSpec(memory_space=pltpu.SMEM)
    message = (samples * channels // LANES, LANES)
    anywhere = pl.BlockSpec(memory_space=pl.ANY)
    slots = 4 * max(n_lat, n_lon)
    taps = (9 * channels, channels)

    def padded(d):
        shape = (rows + 2 * d, (cols + 2 * d) * samples, channels)
        return pltpu.VMEM(shape, jnp.bfloat16)

    ordered = pl.pallas_call(
        functools.partial(kernel, n_lat, n_lon, rows, cols, samples, channels),
        out_shape=jax.ShapeDtypeStruct((rows, cols * samples, channels), jnp.bfloat16),
        in_specs=[anywhere, smem, vmem, anywhere, anywhere],
        out_specs=vmem,
        scratch_shapes=[
            pltpu.VMEM(features.shape, jnp.bfloat16),
            pltpu.VMEM(taps, jnp.bfloat16),
            pltpu.VMEM(taps, jnp.bfloat16),
            padded(d1),
            padded(d2),
            pltpu.VMEM((samples, channels), jnp.float32),
            pltpu.VMEM((2, 2) + message, jnp.float32),
            pltpu.VMEM((2, n_lat) + message, jnp.float32),
            pltpu.VMEM((2, n_lon) + message, jnp.float32),
            pltpu.SemaphoreType.DMA((LOAD_CHUNKS + 2,)),
            pltpu.SemaphoreType.DMA((slots,)),
            pltpu.SemaphoreType.DMA((slots,)),
            pltpu.SemaphoreType.DMA((16,)),
            pltpu.SemaphoreType.DMA((16,)),
        ],
        compiler_params=pltpu.CompilerParams(
            collective_id=0, has_side_effects=True, vmem_limit_bytes=56 * 2**20
        ),
    )(
        features,
        band_points,
        survival_flags,
        first_weight.reshape(taps),
        second_weight.reshape(taps),
    )
    return pl.pallas_call(
        reorder,
        grid=(rows // ROWS_PER_STEP,),
        out_shape=jax.ShapeDtypeStruct(features.shape, jnp.bfloat16),
        in_specs=[pl.BlockSpec((ROWS_PER_STEP, cols * samples, channels), lambda i: (i, 0, 0))],
        out_specs=pl.BlockSpec((samples, ROWS_PER_STEP, cols, channels), lambda i: (0, i, 0, 0)),
    )(ordered)


def solution(mesh):
    in_specs = (P(None, "lat", "lon", None), P(), P(), P(), P())
    out_specs = P(None, "lat", "lon", None)
    return jax.shard_map(
        functools.partial(per_device, mesh.shape["lat"], mesh.shape["lon"]),
        mesh=mesh,
        in_specs=in_specs,
        out_specs=out_specs,
        check_vma=False,
    )
```

```python
import functools

import jax
import jax.numpy as jnp
from jax import lax
from jax.experimental import pallas as pl
from jax.experimental.pallas import tpu as pltpu
from jax.sharding import PartitionSpec as P

GROUPS = 32
DILATIONS = (2, 4)
EPS = 1e-05
KEEP_RATE = 0.8
LANES = 128
LOAD_CHUNKS = 4
REORDER_ROWS = 8
MESH = pl.DeviceIdType.MESH


def permutation(outer, inner, dtype):
    size = outer * inner
    row = lax.broadcasted_iota(jnp.int32, (size, size), 0)
    col = lax.broadcasted_iota(jnp.int32, (size, size), 1)
    wanted = lax.rem(row, inner) * outer + row // inner
    return (col == wanted).astype(jnp.float32).astype(dtype)


def kernel(
    n_lat, n_lon, tile_rows, tile_cols, samples, channels,
    feat_hbm, points_ref, flags_ref, w1_hbm, w2_hbm, x_ref,
    feat_ref, w1_ref, w2_ref, pad1, pad2, total_ref, mine, lat_slots, lon_slots,
    local_sem, stat_send, stat_recv, halo_send, halo_recv,
):
    cells = tile_cols * samples
    group_size = channels // GROUPS
    lat = lax.axis_index("lat")
    lon = lax.axis_index("lon")
    row0 = lat * tile_rows
    col0 = lon * tile_cols

    chunk = tile_rows // LOAD_CHUNKS
    loads = []
    for c in range(LOAD_CHUNKS):
        part = (slice(None), pl.ds(c * chunk, chunk))
        loads.append((feat_hbm.at[part], feat_ref.at[part]))
    loads += [(w1_hbm, w1_ref), (w2_hbm, w2_ref)]
    loads = [pltpu.make_async_copy(*ends, local_sem.at[k]) for k, ends in enumerate(loads)]
    for copy in loads:
        copy.start()

    barrier = pltpu.get_barrier_semaphore()
    for k in range(1, n_lat):
        pl.semaphore_signal(
            barrier, inc=1, device_id={"lat": lax.rem(lat + k, n_lat)}, device_id_type=MESH
        )
    for k in range(1, n_lon):
        pl.semaphore_signal(
            barrier, inc=1, device_id={"lon": lax.rem(lon + k, n_lon)}, device_id_type=MESH
        )

    lat_total = tile_rows * n_lat
    lon_total = tile_cols * n_lon

    def live(row, first, width):
        shape = (width // samples, samples, channels)
        start = lax.rem(col0 + first // samples + lon_total, lon_total)
        place = row0 + row
        points = points_ref[jnp.clip(place, 0, lat_total - 1)]
        points = jnp.where((place >= 0) & (place < lat_total), points, 0)
        return lax.broadcasted_iota(jnp.int32, shape, 0) + start < points

    def cubed(values):
        return values.reshape(-1, samples, channels)

    halves = channels // LANES

    def pack(values):
        return jnp.concatenate(jnp.split(values, halves, axis=1), axis=0)

    def unpack(values):
        return jnp.concatenate(jnp.split(values, halves, axis=0), axis=1)

    lane = lax.broadcasted_iota(jnp.int32, (halves * samples, LANES), 1)
    place = lane % group_size

    def group_total(values):
        step = 1
        while step < group_size:
            above = pltpu.roll(values, LANES - step, 1)
            below = pltpu.roll(values, step, 1)
            values = values + jnp.where((lane & step) == 0, above, below)
            step *= 2
        return values

    def spread(values):
        return unpack(group_total(jnp.where(place == 0, values, 0.0)))

    def message(total, squares, count):
        return jnp.where(place == 0, total, jnp.where(place == 1, squares, count))

    def count_row(i, total):
        return total + jnp.clip(points_ref[row0 + i] - col0, 0, tile_cols)

    local_cells = lax.fori_loop(0, tile_rows, count_row, jnp.int32(0))
    local_count = jnp.full((halves * samples, LANES), local_cells * group_size, jnp.int32).astype(
        jnp.float32
    )

    def combine(parts):
        total = sum(p[0] for p in parts)
        count = sum(p[2] for p in parts)
        mean = total / jnp.maximum(count, 1.0)
        spreads = None
        for p in parts:
            gap = p[0] / jnp.maximum(p[2], 1.0) - mean
            term = p[1] + p[2] * gap * gap
            spreads = term if spreads is None else spreads + term
        return total, spreads, count, mean

    def exchange(round_index, stage, axis, index, peers, slots):
        copies = []
        base = (round_index * 2 + stage) * max(n_lat, n_lon)
        for k in range(1, peers):
            copy = pltpu.make_async_remote_copy(
                src_ref=mine.at[round_index, stage],
                dst_ref=slots.at[round_index, k],
                send_sem=stat_send.at[base + k],
                recv_sem=stat_recv.at[base + k],
                device_id={axis: lax.rem(index + k, peers)},
                device_id_type=MESH,
            )
            copy.start()
            copies.append(copy)
        for copy in copies:
            copy.wait()
        packed = [mine[round_index, stage]] + [slots[round_index, k] for k in range(1, peers)]
        return combine(
            [(p, pltpu.roll(p, LANES - 1, 1), pltpu.roll(p, LANES - 2, 1)) for p in packed]
        )

    by_column = permutation(tile_cols, samples, jnp.bfloat16)

    def load_row(i, total):
        values = feat_ref[:, i].reshape(cells, channels)
        values = jnp.dot(by_column, values, preferred_element_type=jnp.float32)
        x_ref[i] = values.astype(jnp.bfloat16)
        return total + jnp.where(live(i, 0, cells), cubed(values), 0.0).sum(axis=0)

    def local_statistics(round_index, channel_total):
        total = group_total(pack(channel_total))
        mean = unpack(total / jnp.maximum(local_count, 1.0))

        def square_row(i, acc):
            gap = cubed(x_ref[i].astype(jnp.float32)) - mean[None]
            return acc + jnp.where(live(i, 0, cells), gap * gap, 0.0).sum(axis=0)

        zero = jnp.zeros((samples, channels), jnp.float32)
        squares = group_total(pack(lax.fori_loop(0, tile_rows, square_row, zero)))
        mine[round_index, 0] = message(total, squares, local_count)

    def global_statistics(round_index):
        total, squares, count, _ = exchange(round_index, 0, "lat", lat, n_lat, lat_slots)
        mine[round_index, 1] = message(
            total, pltpu.roll(squares, 1, 1), pltpu.roll(count, 2, 1)
        )
        total, squares, count, mean = exchange(round_index, 1, "lon", lon, n_lon, lon_slots)
        inv_std = lax.rsqrt(squares / jnp.maximum(count, 1.0) + EPS)
        return spread(mean), spread(inv_std) * 0.5

    pads = (pad1, pad2)
    up = {"lat": lax.rem(lat + n_lat - 1, n_lat)}
    down = {"lat": lax.rem(lat + 1, n_lat)}
    right = {"lon": lax.rem(lon + 1, n_lon)}
    left = {"lon": lax.rem(lon + n_lon - 1, n_lon)}

    def halo_copies(round_index):
        d = DILATIONS[round_index]
        side = d * samples
        rows = tile_rows
        pad = pads[round_index]
        centre = pl.ds(side, cells)

        def remote(number, src, dst, target):
            return pltpu.make_async_remote_copy(
                src_ref=src,
                dst_ref=dst,
                send_sem=halo_send.at[round_index * 8 + number],
                recv_sem=halo_recv.at[round_index * 8 + number],
                device_id=target,
                device_id_type=MESH,
            )

        to_up = remote(0, x_ref.at[pl.ds(0, d)], pad.at[pl.ds(d + rows, d), centre], up)
        to_down = remote(1, x_ref.at[pl.ds(rows - d, d)], pad.at[pl.ds(0, d), centre], down)
        inner = pl.ds(d, rows)
        flanks = [
            remote(
                2, x_ref.at[:, pl.ds(cells - side, side)], pad.at[inner, pl.ds(0, side)], right
            ),
            remote(
                3, x_ref.at[:, pl.ds(0, side)], pad.at[inner, pl.ds(side + cells, side)], left
            ),
        ]
        corners = []
        for number, first in ((4, 0), (6, d + rows)):
            span = pl.ds(first, d)
            corners += [
                remote(
                    number, pad.at[span, pl.ds(cells, side)], pad.at[span, pl.ds(0, side)], right
                ),
                remote(
                    number + 1,
                    pad.at[span, pl.ds(side, side)],
                    pad.at[span, pl.ds(side + cells, side)],
                    left,
                ),
            ]
        return to_up, to_down, flanks, corners

    def send_halos(round_index):
        to_up, to_down, flanks, _ = halo_copies(round_index)
        for copy in flanks:
            copy.start()

        @pl.when(lat > 0)
        def _():
            to_up.start()

        @pl.when(lat < n_lat - 1)
        def _():
            to_down.start()

    def send_corners(round_index):
        to_up, to_down, _, corners = halo_copies(round_index)
        d = DILATIONS[round_index]
        pad = pads[round_index]
        centre = pl.ds(d * samples, cells)
        blank = jnp.zeros((d, cells, channels), jnp.bfloat16)

        @pl.when(lat == 0)
        def _():
            pad[pl.ds(0, d), centre, :] = blank

        @pl.when(lat == n_lat - 1)
        def _():
            pad[pl.ds(d + tile_rows, d), centre, :] = blank

        @pl.when(lat > 0)
        def _():
            to_down.wait_recv()
            to_up.wait_send()

        @pl.when(lat < n_lat - 1)
        def _():
            to_up.wait_recv()
            to_down.wait_send()

        for copy in corners:
            copy.start()

    def wait_halos(round_index):
        _, _, flanks, corners = halo_copies(round_index)
        for copy in flanks + corners:
            copy.wait()

    def block(round_index, w_ref, weight_load, ahead, mean, half_scale):
        d = DILATIONS[round_index]
        side = d * samples
        pad = pads[round_index]

        def act(i, first, width, own):
            spot = (d + i, pl.ds(side + first, width), slice(None))
            values = x_ref[i, pl.ds(first, width), :] if own else pad[spot]
            values = cubed(values.astype(jnp.float32))
            half = (values - mean[None]) * half_scale[None]
            hidden = half * jnp.tanh(half) + half
            hidden = jnp.where(live(i, first, width), hidden, 0.0).reshape(width, channels)
            pad[spot] = hidden.astype(jnp.bfloat16)

        square = (samples, samples)
        flag = jnp.broadcast_to(
            flags_ref[round_index : round_index + 1, :].astype(jnp.float32), square
        )
        own = lax.broadcasted_iota(jnp.int32, square, 0) == lax.broadcasted_iota(
            jnp.int32, square, 1
        )
        flag = jnp.where(own, flag, 0.0).sum(axis=1, keepdims=True)
        kept = jnp.broadcast_to(flag, (samples, channels)) / KEEP_RATE

        def conv(first_row, height, first, width):
            taps = [
                pad[
                    pl.ds(first_row + r * d, height), pl.ds(first + c * side, width), :
                ].reshape(height * width, channels)
                for r in range(3)
                for c in range(3)
            ]
            summed = jnp.dot(
                jnp.concatenate(taps, axis=1), w_ref[...], preferred_element_type=jnp.float32
            )
            summed = (cubed(summed) * kept[None]).reshape(height, width, channels)
            where = (pl.ds(first_row, height), pl.ds(first, width), slice(None))
            new = (x_ref[where].astype(jnp.float32) + summed).astype(jnp.bfloat16)
            x_ref[where] = new
            if round_index == 0:
                total = total_ref[...]
                for k in range(height):
                    values = cubed(new[k].astype(jnp.float32))
                    mask = live(first_row + k, first, width)
                    total = total + jnp.where(mask, values, 0.0).sum(axis=0)
                total_ref[...] = total

        edge = max(DILATIONS)
        edge_cells = edge * samples
        steps = tile_rows // edge

        def inner(step):
            conv(step * edge, edge, edge_cells, cells - 2 * edge_cells)

        send_corners(round_index)

        @pl.loop(0, tile_rows)
        def _(i):
            act(i, 0, cells, True)

        weight_load.wait()
        pl.loop(1, 1 + ahead)(inner)
        wait_halos(round_index)

        @pl.loop(0, tile_rows)
        def _(i):
            act(i, -side, side, False)
            act(i, cells, side, False)

        @pl.loop(0, 2 * d)
        def _(k):
            i = jnp.where(k < d, k - d, tile_rows + k - d)
            act(i, -side, side, False)
            act(i, 0, cells, False)
            act(i, cells, side, False)

        @pl.loop(0, 2)
        def _(k):
            conv(k * (tile_rows - edge), edge, 0, cells)

        @pl.loop(0, 2)
        def _(k):
            first = pl.multiple_of(k * (cells - edge_cells), edge_cells)
            conv(edge, tile_rows - 2 * edge, first, edge_cells)

        if round_index == 0:
            send_halos(1)
        if ahead < steps - 2:
            pl.loop(1 + ahead, steps - 1)(inner)

    total = jnp.zeros((samples, channels), jnp.float32)
    total_ref[...] = total
    for c in range(LOAD_CHUNKS):
        loads[c].wait()
        total = lax.fori_loop(c * chunk, (c + 1) * chunk, load_row, total)
    pl.semaphore_wait(barrier, n_lat - 1 + n_lon - 1)
    send_halos(0)
    local_statistics(0, total)
    block(0, w1_ref, loads[LOAD_CHUNKS], 2, *global_statistics(0))
    local_statistics(1, total_ref[...])
    last = tile_rows // max(DILATIONS) - 2
    block(1, w2_ref, loads[LOAD_CHUNKS + 1], last, *global_statistics(1))


def reorder(x_ref, out_ref):
    samples, rows, cols, channels = out_ref.shape
    by_sample = permutation(samples, cols, jnp.bfloat16)
    for i in range(rows):
        values = jnp.dot(by_sample, x_ref[i], preferred_element_type=jnp.float32)
        out_ref[:, i] = values.astype(jnp.bfloat16).reshape(samples, cols, channels)


def per_device(n_lat, n_lon, features, band_points, survival_flags, first_weight, second_weight):
    samples, rows, cols, channels = features.shape
    d1, d2 = DILATIONS
    vmem = pl.BlockSpec(memory_space=pltpu.VMEM)
    smem = pl.BlockSpec(memory_space=pltpu.SMEM)
    message = (samples * channels // LANES, LANES)
    anywhere = pl.BlockSpec(memory_space=pl.ANY)
    slots = 4 * max(n_lat, n_lon)
    taps = (9 * channels, channels)

    def padded(d):
        shape = (rows + 2 * d, (cols + 2 * d) * samples, channels)
        return pltpu.VMEM(shape, jnp.bfloat16)

    ordered = pl.pallas_call(
        functools.partial(kernel, n_lat, n_lon, rows, cols, samples, channels),
        out_shape=jax.ShapeDtypeStruct((rows, cols * samples, channels), jnp.bfloat16),
        in_specs=[anywhere, smem, vmem, anywhere, anywhere],
        out_specs=vmem,
        scratch_shapes=[
            pltpu.VMEM(features.shape, jnp.bfloat16),
            pltpu.VMEM(taps, jnp.bfloat16),
            pltpu.VMEM(taps, jnp.bfloat16),
            padded(d1),
            padded(d2),
            pltpu.VMEM((samples, channels), jnp.float32),
            pltpu.VMEM((2, 2) + message, jnp.float32),
            pltpu.VMEM((2, n_lat) + message, jnp.float32),
            pltpu.VMEM((2, n_lon) + message, jnp.float32),
            pltpu.SemaphoreType.DMA((LOAD_CHUNKS + 2,)),
            pltpu.SemaphoreType.DMA((slots,)),
            pltpu.SemaphoreType.DMA((slots,)),
            pltpu.SemaphoreType.DMA((16,)),
            pltpu.SemaphoreType.DMA((16,)),
        ],
        compiler_params=pltpu.CompilerParams(
            collective_id=0, has_side_effects=True, vmem_limit_bytes=56 * 2**20
        ),
    )(
        features,
        band_points,
        survival_flags.T,
        first_weight.reshape(taps),
        second_weight.reshape(taps),
    )
    return pl.pallas_call(
        reorder,
        grid=(rows // REORDER_ROWS,),
        out_shape=jax.ShapeDtypeStruct(features.shape, jnp.bfloat16),
        in_specs=[pl.BlockSpec((REORDER_ROWS, cols * samples, channels), lambda i: (i, 0, 0))],
        out_specs=pl.BlockSpec((samples, REORDER_ROWS, cols, channels), lambda i: (0, i, 0, 0)),
    )(ordered)


def solution(mesh):
    in_specs = (P(None, "lat", "lon", None), P(), P(), P(), P())
    out_specs = P(None, "lat", "lon", None)
    return jax.shard_map(
        functools.partial(per_device, mesh.shape["lat"], mesh.shape["lon"]),
        mesh=mesh,
        in_specs=in_specs,
        out_specs=out_specs,
        check_vma=False,
    )
```

```python
import functools

import jax
import jax.numpy as jnp
from jax import lax
from jax.experimental import pallas as pl
from jax.experimental.pallas import tpu as pltpu
from jax.sharding import PartitionSpec as P

GROUPS = 32
DILATIONS = (2, 4)
EPS = 1e-05
KEEP_RATE = 0.8
LANES = 128
LOAD_CHUNKS = 4
REORDER_ROWS = 8
MESH = pl.DeviceIdType.MESH


def permutation(outer, inner, dtype):
    size = outer * inner
    row = lax.broadcasted_iota(jnp.int32, (size, size), 0)
    col = lax.broadcasted_iota(jnp.int32, (size, size), 1)
    wanted = lax.rem(row, inner) * outer + row // inner
    return (col == wanted).astype(jnp.float32).astype(dtype)


def kernel(
    n_lat, n_lon, tile_rows, tile_cols, samples, channels,
    feat_hbm, points_ref, flags_ref, w1_hbm, w2_hbm, x_ref,
    feat_ref, w1_ref, w2_ref, pad1, pad2, total_ref, mine, lat_slots, lon_slots,
    local_sem, stat_send, stat_recv, halo_send, halo_recv,
):
    cells = tile_cols * samples
    group_size = channels // GROUPS
    lat = lax.axis_index("lat")
    lon = lax.axis_index("lon")
    row0 = lat * tile_rows
    col0 = lon * tile_cols

    chunk = tile_rows // LOAD_CHUNKS
    loads = []
    for c in range(LOAD_CHUNKS):
        part = (slice(None), pl.ds(c * chunk, chunk))
        loads.append((feat_hbm.at[part], feat_ref.at[part]))
    loads += [(w1_hbm, w1_ref), (w2_hbm, w2_ref)]
    loads = [pltpu.make_async_copy(*ends, local_sem.at[k]) for k, ends in enumerate(loads)]
    for copy in loads:
        copy.start()

    barrier = pltpu.get_barrier_semaphore()
    for k in range(1, n_lat):
        pl.semaphore_signal(
            barrier, inc=1, device_id={"lat": lax.rem(lat + k, n_lat)}, device_id_type=MESH
        )
    for k in range(1, n_lon):
        pl.semaphore_signal(
            barrier, inc=1, device_id={"lon": lax.rem(lon + k, n_lon)}, device_id_type=MESH
        )

    lat_total = tile_rows * n_lat
    lon_total = tile_cols * n_lon

    def live(row, first, width):
        shape = (width // samples, samples, channels)
        start = lax.rem(col0 + first // samples + lon_total, lon_total)
        place = row0 + row
        points = points_ref[jnp.clip(place, 0, lat_total - 1)]
        points = jnp.where((place >= 0) & (place < lat_total), points, 0)
        return lax.broadcasted_iota(jnp.int32, shape, 0) + start < points

    def cubed(values):
        return values.reshape(-1, samples, channels)

    halves = channels // LANES

    def pack(values):
        return jnp.concatenate(jnp.split(values, halves, axis=1), axis=0)

    def unpack(values):
        return jnp.concatenate(jnp.split(values, halves, axis=0), axis=1)

    lane = lax.broadcasted_iota(jnp.int32, (halves * samples, LANES), 1)
    place = lane % group_size

    def group_total(values):
        step = 1
        while step < group_size:
            above = pltpu.roll(values, LANES - step, 1)
            below = pltpu.roll(values, step, 1)
            values = values + jnp.where((lane & step) == 0, above, below)
            step *= 2
        return values

    def spread(values):
        return unpack(group_total(jnp.where(place == 0, values, 0.0)))

    def message(total, squares, count):
        return jnp.where(place == 0, total, jnp.where(place == 1, squares, count))

    def count_row(i, total):
        return total + jnp.clip(points_ref[row0 + i] - col0, 0, tile_cols)

    local_cells = lax.fori_loop(0, tile_rows, count_row, jnp.int32(0))
    local_count = jnp.full((halves * samples, LANES), local_cells * group_size, jnp.int32).astype(
        jnp.float32
    )

    def combine(parts):
        total = sum(p[0] for p in parts)
        count = sum(p[2] for p in parts)
        mean = total / jnp.maximum(count, 1.0)
        spreads = None
        for p in parts:
            gap = p[0] / jnp.maximum(p[2], 1.0) - mean
            term = p[1] + p[2] * gap * gap
            spreads = term if spreads is None else spreads + term
        return total, spreads, count, mean

    def exchange(round_index, stage, axis, index, peers, slots):
        copies = []
        base = (round_index * 2 + stage) * max(n_lat, n_lon)
        for k in range(1, peers):
            copy = pltpu.make_async_remote_copy(
                src_ref=mine.at[round_index, stage],
                dst_ref=slots.at[round_index, k],
                send_sem=stat_send.at[base + k],
                recv_sem=stat_recv.at[base + k],
                device_id={axis: lax.rem(index + k, peers)},
                device_id_type=MESH,
            )
            copy.start()
            copies.append(copy)
        for copy in copies:
            copy.wait()
        packed = [mine[round_index, stage]] + [slots[round_index, k] for k in range(1, peers)]
        return combine(
            [(p, pltpu.roll(p, LANES - 1, 1), pltpu.roll(p, LANES - 2, 1)) for p in packed]
        )

    by_column = permutation(tile_cols, samples, jnp.bfloat16)

    def load_row(i, total):
        values = feat_ref[:, i].reshape(cells, channels)
        values = jnp.dot(by_column, values, preferred_element_type=jnp.float32)
        x_ref[i] = values.astype(jnp.bfloat16)
        return total + jnp.where(live(i, 0, cells), cubed(values), 0.0).sum(axis=0)

    def local_statistics(round_index, channel_total):
        total = group_total(pack(channel_total))
        mean = unpack(total / jnp.maximum(local_count, 1.0))

        def square_row(i, acc):
            gap = cubed(x_ref[i].astype(jnp.float32)) - mean[None]
            return acc + jnp.where(live(i, 0, cells), gap * gap, 0.0).sum(axis=0)

        zero = jnp.zeros((samples, channels), jnp.float32)
        squares = group_total(pack(lax.fori_loop(0, tile_rows, square_row, zero)))
        mine[round_index, 0] = message(total, squares, local_count)

    def global_statistics(round_index):
        total, squares, count, _ = exchange(round_index, 0, "lat", lat, n_lat, lat_slots)
        mine[round_index, 1] = message(
            total, pltpu.roll(squares, 1, 1), pltpu.roll(count, 2, 1)
        )
        total, squares, count, mean = exchange(round_index, 1, "lon", lon, n_lon, lon_slots)
        inv_std = lax.rsqrt(squares / jnp.maximum(count, 1.0) + EPS)
        return spread(mean), spread(inv_std) * 0.5

    pads = (pad1, pad2)
    up = {"lat": lax.rem(lat + n_lat - 1, n_lat)}
    down = {"lat": lax.rem(lat + 1, n_lat)}
    right = {"lon": lax.rem(lon + 1, n_lon)}
    left = {"lon": lax.rem(lon + n_lon - 1, n_lon)}

    def halo_copies(round_index):
        d = DILATIONS[round_index]
        side = d * samples
        rows = tile_rows
        pad = pads[round_index]
        centre = pl.ds(side, cells)

        def remote(number, src, dst, target):
            return pltpu.make_async_remote_copy(
                src_ref=src,
                dst_ref=dst,
                send_sem=halo_send.at[round_index * 8 + number],
                recv_sem=halo_recv.at[round_index * 8 + number],
                device_id=target,
                device_id_type=MESH,
            )

        to_up = remote(0, x_ref.at[pl.ds(0, d)], pad.at[pl.ds(d + rows, d), centre], up)
        to_down = remote(1, x_ref.at[pl.ds(rows - d, d)], pad.at[pl.ds(0, d), centre], down)
        inner = pl.ds(d, rows)
        flanks = [
            remote(
                2, x_ref.at[:, pl.ds(cells - side, side)], pad.at[inner, pl.ds(0, side)], right
            ),
            remote(
                3, x_ref.at[:, pl.ds(0, side)], pad.at[inner, pl.ds(side + cells, side)], left
            ),
        ]
        corners = []
        for number, first in ((4, 0), (6, d + rows)):
            span = pl.ds(first, d)
            corners += [
                remote(
                    number, pad.at[span, pl.ds(cells, side)], pad.at[span, pl.ds(0, side)], right
                ),
                remote(
                    number + 1,
                    pad.at[span, pl.ds(side, side)],
                    pad.at[span, pl.ds(side + cells, side)],
                    left,
                ),
            ]
        return to_up, to_down, flanks, corners

    def send_halos(round_index):
        to_up, to_down, flanks, _ = halo_copies(round_index)
        for copy in flanks:
            copy.start()

        @pl.when(lat > 0)
        def _():
            to_up.start()

        @pl.when(lat < n_lat - 1)
        def _():
            to_down.start()

    def send_corners(round_index):
        to_up, to_down, _, corners = halo_copies(round_index)
        d = DILATIONS[round_index]
        pad = pads[round_index]
        centre = pl.ds(d * samples, cells)
        blank = jnp.zeros((d, cells, channels), jnp.bfloat16)

        @pl.when(lat == 0)
        def _():
            pad[pl.ds(0, d), centre, :] = blank

        @pl.when(lat == n_lat - 1)
        def _():
            pad[pl.ds(d + tile_rows, d), centre, :] = blank

        @pl.when(lat > 0)
        def _():
            to_down.wait_recv()
            to_up.wait_send()

        @pl.when(lat < n_lat - 1)
        def _():
            to_up.wait_recv()
            to_down.wait_send()

        for copy in corners:
            copy.start()

    def wait_halos(round_index):
        _, _, flanks, corners = halo_copies(round_index)
        for copy in flanks + corners:
            copy.wait()

    def block(round_index, w_ref, weight_load, ahead, mean, half_scale):
        d = DILATIONS[round_index]
        side = d * samples
        pad = pads[round_index]

        def act(i, first, width, own):
            spot = (d + i, pl.ds(side + first, width), slice(None))
            values = x_ref[i, pl.ds(first, width), :] if own else pad[spot]
            values = cubed(values.astype(jnp.float32))
            half = (values - mean[None]) * half_scale[None]
            hidden = half * jnp.tanh(half) + half
            hidden = jnp.where(live(i, first, width), hidden, 0.0).reshape(width, channels)
            pad[spot] = hidden.astype(jnp.bfloat16)

        square = (samples, samples)
        flag = jnp.broadcast_to(
            flags_ref[round_index : round_index + 1, :].astype(jnp.float32), square
        )
        own = lax.broadcasted_iota(jnp.int32, square, 0) == lax.broadcasted_iota(
            jnp.int32, square, 1
        )
        flag = jnp.where(own, flag, 0.0).sum(axis=1, keepdims=True)
        kept = jnp.broadcast_to(flag, (samples, channels)) / KEEP_RATE

        def conv(first_row, height, first, width):
            summed = None
            for r in range(3):
                for c in range(3):
                    tap = pad[
                        pl.ds(first_row + r * d, height), pl.ds(first + c * side, width), :
                    ].reshape(height * width, channels)
                    weight = w_ref[pl.ds((3 * r + c) * channels, channels), :]
                    term = jnp.dot(tap, weight, preferred_element_type=jnp.float32)
                    summed = term if summed is None else summed + term
            summed = (cubed(summed) * kept[None]).reshape(height, width, channels)
            where = (pl.ds(first_row, height), pl.ds(first, width), slice(None))
            new = (x_ref[where].astype(jnp.float32) + summed).astype(jnp.bfloat16)
            x_ref[where] = new
            if round_index == 0:
                total = total_ref[...]
                for k in range(height):
                    values = cubed(new[k].astype(jnp.float32))
                    mask = live(first_row + k, first, width)
                    total = total + jnp.where(mask, values, 0.0).sum(axis=0)
                total_ref[...] = total

        edge = max(DILATIONS)
        edge_cells = edge * samples
        steps = tile_rows // edge

        def inner(step):
            conv(step * edge, edge, edge_cells, cells - 2 * edge_cells)

        send_corners(round_index)

        @pl.loop(0, tile_rows)
        def _(i):
            act(i, 0, cells, True)

        weight_load.wait()
        pl.loop(1, 1 + ahead)(inner)
        wait_halos(round_index)

        @pl.loop(0, tile_rows)
        def _(i):
            act(i, -side, side, False)
            act(i, cells, side, False)

        @pl.loop(0, 2 * d)
        def _(k):
            i = jnp.where(k < d, k - d, tile_rows + k - d)
            act(i, -side, side, False)
            act(i, 0, cells, False)
            act(i, cells, side, False)

        @pl.loop(0, 2)
        def _(k):
            conv(k * (tile_rows - edge), edge, 0, cells)

        @pl.loop(0, 2)
        def _(k):
            first = pl.multiple_of(k * (cells - edge_cells), edge_cells)
            conv(edge, tile_rows - 2 * edge, first, edge_cells)

        if round_index == 0:
            send_halos(1)
        if ahead < steps - 2:
            pl.loop(1 + ahead, steps - 1)(inner)

    total = jnp.zeros((samples, channels), jnp.float32)
    total_ref[...] = total
    for c in range(LOAD_CHUNKS):
        loads[c].wait()
        total = lax.fori_loop(c * chunk, (c + 1) * chunk, load_row, total)
    pl.semaphore_wait(barrier, n_lat - 1 + n_lon - 1)
    send_halos(0)
    local_statistics(0, total)
    block(0, w1_ref, loads[LOAD_CHUNKS], 2, *global_statistics(0))
    local_statistics(1, total_ref[...])
    last = tile_rows // max(DILATIONS) - 2
    block(1, w2_ref, loads[LOAD_CHUNKS + 1], last, *global_statistics(1))


def reorder(x_ref, out_ref):
    samples, rows, cols, channels = out_ref.shape
    by_sample = permutation(samples, cols, jnp.bfloat16)
    for i in range(rows):
        values = jnp.dot(by_sample, x_ref[i], preferred_element_type=jnp.float32)
        out_ref[:, i] = values.astype(jnp.bfloat16).reshape(samples, cols, channels)


def per_device(n_lat, n_lon, features, band_points, survival_flags, first_weight, second_weight):
    samples, rows, cols, channels = features.shape
    d1, d2 = DILATIONS
    vmem = pl.BlockSpec(memory_space=pltpu.VMEM)
    smem = pl.BlockSpec(memory_space=pltpu.SMEM)
    message = (samples * channels // LANES, LANES)
    anywhere = pl.BlockSpec(memory_space=pl.ANY)
    slots = 4 * max(n_lat, n_lon)
    taps = (9 * channels, channels)

    def padded(d):
        shape = (rows + 2 * d, (cols + 2 * d) * samples, channels)
        return pltpu.VMEM(shape, jnp.bfloat16)

    ordered = pl.pallas_call(
        functools.partial(kernel, n_lat, n_lon, rows, cols, samples, channels),
        out_shape=jax.ShapeDtypeStruct((rows, cols * samples, channels), jnp.bfloat16),
        in_specs=[anywhere, smem, vmem, anywhere, anywhere],
        out_specs=vmem,
        scratch_shapes=[
            pltpu.VMEM(features.shape, jnp.bfloat16),
            pltpu.VMEM(taps, jnp.bfloat16),
            pltpu.VMEM(taps, jnp.bfloat16),
            padded(d1),
            padded(d2),
            pltpu.VMEM((samples, channels), jnp.float32),
            pltpu.VMEM((2, 2) + message, jnp.float32),
            pltpu.VMEM((2, n_lat) + message, jnp.float32),
            pltpu.VMEM((2, n_lon) + message, jnp.float32),
            pltpu.SemaphoreType.DMA((LOAD_CHUNKS + 2,)),
            pltpu.SemaphoreType.DMA((slots,)),
            pltpu.SemaphoreType.DMA((slots,)),
            pltpu.SemaphoreType.DMA((16,)),
            pltpu.SemaphoreType.DMA((16,)),
        ],
        compiler_params=pltpu.CompilerParams(
            collective_id=0, has_side_effects=True, vmem_limit_bytes=56 * 2**20
        ),
    )(
        features,
        band_points,
        survival_flags.T,
        first_weight.reshape(taps),
        second_weight.reshape(taps),
    )
    return pl.pallas_call(
        reorder,
        grid=(rows // REORDER_ROWS,),
        out_shape=jax.ShapeDtypeStruct(features.shape, jnp.bfloat16),
        in_specs=[pl.BlockSpec((REORDER_ROWS, cols * samples, channels), lambda i: (i, 0, 0))],
        out_specs=pl.BlockSpec((samples, REORDER_ROWS, cols, channels), lambda i: (0, i, 0, 0)),
    )(ordered)


def solution(mesh):
    in_specs = (P(None, "lat", "lon", None), P(), P(), P(), P())
    out_specs = P(None, "lat", "lon", None)
    return jax.shard_map(
        functools.partial(per_device, mesh.shape["lat"], mesh.shape["lon"]),
        mesh=mesh,
        in_specs=in_specs,
        out_specs=out_specs,
        check_vma=False,
    )
```
